32 devices in a mesh: groups: 2 (over y), dp: 8 (over z, x), shard: 2 (over core).
Axes of the slice: x: 2, y: 2, z: 4, core: 2. Of those that a mesh axis runs over, the one named last changes fastest.
Arguments:
- projected: bfloat16 [8192, 4096], P(('groups', 'dp', 'shard')), parts along dimension 0, may hold values from -6 to 6
- grad_gated: bfloat16 [8192, 1024], P(('groups', 'dp', 'shard')), parts along dimension 0, may hold values from -6 to 6
- lengths: int32 [170], P('groups'), parts along dimension 0, may hold values from 1 to 96, 4096 in all
Outputs:
- grad_projected: bfloat16 [8192, 4096], P(('groups', 'dp', 'shard')), parts along dimension 0
The draws below stay inside these ranges and needn't reach their ends.
There are 2 independent parts, one for each index of `groups`. The reference program is written for one: setup_inputs(seed, part) draws one part's arguments, and reference() takes and returns one part's arrays. A program takes and returns all parts, laid end to end along the dimension named above; each array names one. Nothing has to cross between parts.
Inputs may be any that keep to these rules, and one draw needn't show every extreme that they name: The lengths sum to 4096 and the longest is exactly 96.
All inputs are finite; a program needn't handle non-finite values.
Results may differ from the reference program's by a relative error of at most 0.0055.
Values may be sent and summed in bfloat16 or wider, within the bound.
A program may use at most 64 MiB of HBM per device.

```python
import math
import jax
import jax.numpy as jnp
import numpy as np
from jax import lax

D = 1024
HEADS = 16
TOK_DEV = 256
MAXLEN = 96
TOKENS = 4096
NSEQ = 85
N_DP = 8
N_SHARD = 2


def block_levels(own_key, extent, split, smallest, high):
    loudness = 1.0
    for position, shards_of in split:
        draws = jax.random.uniform(jax.random.fold_in(jax.random.fold_in(own_key, 6), position), (shards_of,), jnp.float32, smallest / len(split), high / len(split))
        loudness = loudness * jnp.repeat(jnp.exp(draws), extent[position] // shards_of).reshape((-1,) + (1,) * (len(extent) - 1 - position))
    return loudness


def length_profile(number_of, total, most, skew):
    portions = [(1 << 20) // math.isqrt(standing ** skew) + 1 for standing in range(2, number_of + 1)]
    surplus, counts = total - most - (number_of - 1), [1] * (number_of - 1)
    while surplus > 0:
        free = [i for i in range(number_of - 1) if counts[i] < most]
        mass, remaining = sum([portions[i] for i in free]), surplus
        for i in free:
            addition = min(most - counts[i], max(1, remaining * portions[i] // mass), surplus)
            counts[i] = counts[i] + addition
            surplus = surplus - addition
    return np.array([most] + counts)


def uneven_parts(rng, amount, total, bound, skew):
    if amount == 2:
        one = jax.random.randint(rng, (), max(1, total - bound), min(bound, total - 1) + 1)
        return jnp.stack([one, total - one])
    sizes = jnp.asarray(length_profile(amount, total, bound, skew), jnp.int32)
    twos = (amount - 1) // 2
    donor, receiver = sizes[1:1 + 2 * twos:2], sizes[2:2 + 2 * twos:2]
    room = jnp.minimum(donor - 1, bound - receiver)
    passed = jax.random.randint(jax.random.fold_in(rng, 1), (twos,), 0, 1 << 20) % (room + 1)
    sizes = sizes.at[1:1 + 2 * twos:2].set(donor - passed).at[2:2 + 2 * twos:2].set(receiver + passed)
    return sizes[jax.random.permutation(jax.random.fold_in(rng, 2), amount)]


def noise(stream_key, dims, scale, reach, shards=(), held_as=jnp.bfloat16):
    result = scale * jax.random.normal(stream_key, dims, jnp.float32)
    if shards:
        result = result * block_levels(stream_key, dims, shards, -0.22, 0.18)
    return jnp.clip(result, -reach, reach).astype(held_as)


def setup_inputs(seed: int = 0, part: int = 0) -> dict:
    keys = jax.random.split(jax.random.key(seed), 4)
    part_splits = jax.random.split(jax.random.fold_in(keys[3], part), 4)
    return {
        "projected": noise(part_splits[0], (TOKENS, 4 * D), 1.0, 6.0, ((0, 16),)),
        "grad_gated": noise(part_splits[1], (TOKENS, D), 1.0, 6.0, ((0, 16),)),
        "lengths": uneven_parts(part_splits[2], NSEQ, TOKENS, MAXLEN, 2).astype(jnp.int32),
    }


def layout(window_start, own_start, own_count, total_rows, seq_ends):
    positions = window_start + jnp.arange(total_rows, dtype=jnp.int32)
    earlier = seq_ends[None, :] <= positions[:, None]
    seq_start = lax.optimization_barrier(jnp.max(jnp.where(earlier, seq_ends[None, :], jnp.zeros_like(seq_ends)[None, :]), axis=1))
    owned_rows = (seq_start >= own_start) & (seq_start < own_start + own_count) & (positions >= 0)
    same_seq = seq_start[:, None] == seq_start[None, :]
    causal = positions[None, :] <= positions[:, None]
    attn_mask = owned_rows[:, None] & same_seq & causal
    return (owned_rows, attn_mask.astype(jnp.float32))

def local_grads(window, dy_owned, attn_mask):
    width = window.shape[1] // 4
    head_size = width // HEADS
    scale = 1.0 / math.sqrt(head_size)

    def split_heads(matrix):
        return matrix.reshape(-1, HEADS, head_size).transpose(1, 0, 2)
    queries = split_heads(window[:, :width])
    key_rows = split_heads(window[:, width:2 * width])
    value_rows = split_heads(window[:, 2 * width:3 * width])
    gate_rows = window[:, 3 * width:].astype(jnp.float32)

    def head_forward(parts):
        head_query, head_key, head_value = parts
        scores = jnp.dot(head_query, head_key.T, preferred_element_type=jnp.float32) * scale
        weights = (jax.nn.silu(scores) * attn_mask).astype(jnp.bfloat16)
        return jnp.dot(weights, head_value, preferred_element_type=jnp.float32)
    mixed = lax.map(head_forward, (queries, key_rows, value_rows))
    mixed = mixed.transpose(1, 0, 2).reshape(-1, width)
    centered = mixed - lax.optimization_barrier(jnp.mean(mixed, axis=1, keepdims=True))
    variance = lax.optimization_barrier(jnp.mean(centered * centered, axis=1, keepdims=True))
    rstd_rows = lax.rsqrt(variance + 1e-05)
    normed = centered * rstd_rows
    dy_rows = dy_owned.astype(jnp.float32)
    grad_gate = dy_rows * normed
    dnormed = dy_rows * gate_rows
    grad_mixed = rstd_rows * (dnormed - lax.optimization_barrier(jnp.mean(dnormed, axis=1, keepdims=True)) - normed * lax.optimization_barrier(jnp.mean(dnormed * normed, axis=1, keepdims=True)))
    grad_heads = split_heads(grad_mixed.astype(jnp.bfloat16))

    def head_backward(parts):
        head_query, head_key, head_value, head_grad = parts
        scores = jnp.dot(head_query, head_key.T, preferred_element_type=jnp.float32) * scale
        sigmoid_scores = jax.nn.sigmoid(scores)
        weights = (scores * sigmoid_scores * attn_mask).astype(jnp.bfloat16)
        grad_value = jnp.dot(weights.T, head_grad, preferred_element_type=jnp.float32)
        grad_weights = jnp.dot(head_grad, head_value.T, preferred_element_type=jnp.float32)
        slope = sigmoid_scores * (1.0 + scores * (1.0 - sigmoid_scores))
        grad_scores = (grad_weights * attn_mask * slope * scale).astype(jnp.bfloat16)
        grad_query = jnp.dot(grad_scores, head_key, preferred_element_type=jnp.float32)
        grad_key = jnp.dot(grad_scores.T, head_query, preferred_element_type=jnp.float32)
        return (grad_query, grad_key, grad_value)
    grad_query, grad_key, grad_value = lax.map(head_backward, (queries, key_rows, value_rows, grad_heads))

    def merge_heads(stacked):
        return stacked.transpose(1, 0, 2).reshape(-1, width)
    return jnp.concatenate([merge_heads(grad_query), merge_heads(grad_key), merge_heads(grad_value), grad_gate], 1)

def reference(projected, grad_gated, lengths):
    blocks = N_DP * N_SHARD
    seq_ends = jnp.cumsum(lengths).astype(jnp.int32)
    proj_blocks = projected.reshape(blocks, TOK_DEV, 4 * D)
    grad_blocks = grad_gated.reshape(blocks, TOK_DEV, D)
    proj_next = jnp.concatenate([proj_blocks[1:, :MAXLEN], jnp.zeros_like(proj_blocks[:1, :MAXLEN])], 0)
    grad_next = jnp.concatenate([grad_blocks[1:, :MAXLEN], jnp.zeros_like(grad_blocks[:1, :MAXLEN])], 0)

    def advance(tail_grad, inputs):
        block_index, own_proj, next_proj, own_grad, next_grad = inputs
        base_row = block_index * TOK_DEV
        window = jnp.concatenate([own_proj, next_proj], 0)
        dy_window = jnp.concatenate([own_grad, next_grad], 0)
        owned_rows, attn_mask = layout(base_row, base_row, TOK_DEV, TOK_DEV + MAXLEN, seq_ends)
        dy_owned = jnp.where(owned_rows[:, None], dy_window, jnp.zeros_like(dy_window))
        grads = local_grads(window, dy_owned, attn_mask)
        head_part = grads[:MAXLEN] + tail_grad
        own_out = jnp.concatenate([head_part, grads[MAXLEN:TOK_DEV]], 0).astype(jnp.bfloat16)
        return (grads[TOK_DEV:], own_out)
    start_tail = jnp.zeros((MAXLEN, 4 * D), jnp.float32)
    inputs = (jnp.arange(blocks, dtype=jnp.int32), proj_blocks, proj_next, grad_blocks, grad_next)
    last_tail, outputs = lax.scan(advance, start_tail, inputs)
    return outputs.reshape(TOKENS, 4 * D)
```

```python
import functools

import jax
import jax.numpy as jnp
from jax import lax
from jax.experimental import pallas as pl
from jax.experimental.pallas import tpu as pltpu
from jax.sharding import PartitionSpec as P

HEADS = 16
MAXLEN = 96
BLOCK = 64
KEYS = BLOCK + MAXLEN
QUAD = 4
CHUNK = 32
MESH = pl.DeviceIdType.MESH


def dot(a, b, ca, cb):
    return lax.dot_general(a, b, (((ca,), (cb,)), ((), ())), preferred_element_type=jnp.float32)


def kernel(
    n_dp, n_shard,
    proj, grad, lengths, out,
    kv, q, u, dy, mixed, gm, weights, slopes, acc, ones, sixteenths, masks, result,
    outgoing, returned,
    load_sem, store_sem, halo_send, halo_recv, back_send, back_recv,
):
    rows, width = q.shape
    quad = QUAD * (width // HEADS)
    quads = width // quad
    blocks = rows // BLOCK
    tail = rows - MAXLEN
    half = blocks // 2

    me = lax.axis_index("dp") * n_shard + lax.axis_index("shard")
    last = n_dp * n_shard - 1
    has_prev, has_next = me > 0, me < last

    def device(index):
        return {"dp": index // n_shard, "shard": index % n_shard}

    barrier = pltpu.get_barrier_semaphore()

    @pl.when(has_prev)
    def _():
        pl.semaphore_signal(barrier, inc=1, device_id=device(me - 1), device_id_type=MESH)

    @pl.when(has_next)
    def _():
        pl.semaphore_signal(barrier, inc=1, device_id=device(me + 1), device_id_type=MESH)

    def load(i, source, target):
        copy = pltpu.make_async_copy(source, target, load_sem.at[i])
        copy.start()
        return copy

    loads = [
        load(0, proj.at[:, pl.ds(width, 2 * width)], kv.at[pl.ds(MAXLEN, rows), :]),
        load(1, proj.at[:, pl.ds(0, width)], q),
        load(2, proj.at[:, pl.ds(3 * width, width)], u),
        load(3, grad, dy),
    ]

    pl.semaphore_wait(barrier, jnp.where(has_prev, 1, 0) + jnp.where(has_next, 1, 0))

    halo = pltpu.make_async_remote_copy(
        src_ref=proj.at[pl.ds(tail, MAXLEN), pl.ds(width, 2 * width)],
        dst_ref=kv.at[pl.ds(0, MAXLEN), :],
        send_sem=halo_send,
        recv_sem=halo_recv,
        device_id=device(jnp.where(has_next, me + 1, me - 1)),
        device_id_type=MESH,
    )

    @pl.when(has_next)
    def _():
        halo.start()

    @pl.when(jnp.logical_not(has_prev))
    def _():
        kv[pl.ds(0, MAXLEN), :] = jnp.zeros((MAXLEN, 2 * width), kv.dtype)

    @pl.when(jnp.logical_not(has_next))
    def _():
        returned[...] = jnp.zeros_like(returned)

    def backs(c):
        return pltpu.make_async_remote_copy(
            src_ref=outgoing.at[c],
            dst_ref=returned.at[c],
            send_sem=back_send.at[c],
            recv_sem=back_recv.at[c],
            device_id=device(jnp.where(has_prev, me - 1, me + 1)),
            device_id_type=MESH,
        )

    base = (me * rows).astype(jnp.float32)
    lane = (lax.broadcasted_iota(jnp.int32, (1, quad), 1) % BLOCK).astype(jnp.float32)
    positions = [base + float(b * BLOCK) + lane for b in range(blocks)]
    starts = [jnp.zeros((1, quad), jnp.float32) for _ in range(blocks)]
    carry = jnp.zeros((1, 1), jnp.float32)
    count = lengths.shape[1]
    for first in range(0, count, 128):
        span = min(128, count - first)
        part = lengths[:, first : first + span].astype(jnp.float32)
        upto = lax.broadcasted_iota(jnp.int32, (span, span), 1) <= lax.broadcasted_iota(
            jnp.int32, (span, span), 0
        )
        ends = carry + jnp.sum(jnp.where(upto, part, 0.0), axis=1, keepdims=True)
        carry = carry + jnp.sum(part, axis=1, keepdims=True)
        for b in range(blocks):
            reached = jnp.max(jnp.where(ends <= positions[b], ends, 0.0), axis=0, keepdims=True)
            starts[b] = jnp.maximum(starts[b], reached)
    offset = lax.broadcasted_iota(jnp.int32, (KEYS, quad), 0).astype(jnp.float32)
    for b in range(blocks):
        key = offset + (base + float(b * BLOCK - MAXLEN))
        keep = (starts[b] <= key) & (key <= positions[b])
        masks[b] = jnp.where(keep, 1.0, 0.0)

    own_head = (
        lax.broadcasted_iota(jnp.int32, (quad, quad), 0) // BLOCK
        == lax.broadcasted_iota(jnp.int32, (quad, quad), 1) // (quad // QUAD)
    )
    ones[...] = jnp.where(own_head, 1.0, 0.0).astype(ones.dtype)
    sixteenths[...] = jnp.where(own_head, 0.0625, 0.0).astype(ones.dtype)
    left_head = lax.broadcasted_iota(jnp.int32, (BLOCK, quad // 2), 1) < quad // QUAD

    def stacked(value, head_mask):
        return jnp.concatenate([value] * QUAD, 0) * head_mask[...]

    def block_rows(b):
        return pl.ds(b * BLOCK, BLOCK)

    def columns(c, part=0):
        return pl.ds(part * width + c * quad, quad)

    def per_head(transposed, values):
        halves = []
        for p in range(2):
            lanes = slice(p * quad // 2, (p + 1) * quad // 2)
            both = dot(transposed[:, lanes], values[:, lanes], 0, 0)
            halves.append(jnp.where(left_head, both[:BLOCK], both[BLOCK:]))
        return jnp.concatenate(halves, 1)

    def forward(b, c):
        keys = kv[pl.ds(b * BLOCK, KEYS), columns(c)]
        values = kv[pl.ds(b * BLOCK, KEYS), columns(c, 1)]
        queries = stacked(q[block_rows(b), columns(c)], sixteenths)
        h = dot(keys, queries, 1, 1)
        t = jnp.tanh(h)
        kept = (1.0 + t) * masks[b]
        w = (h * kept).astype(weights.dtype)
        weights[b, c] = w
        slopes[b, c] = kept * (1.0 + h * (1.0 - t))
        mixed[block_rows(b), columns(c)] = per_head(w, values)

    def normalise(b):
        at = block_rows(b)
        m = mixed[at, :]
        centered = m - jnp.mean(m, axis=1, keepdims=True)
        rstd = lax.rsqrt(jnp.mean(centered * centered, axis=1, keepdims=True) + 1e-05)
        normed = centered * rstd
        d = dy[at, :].astype(jnp.float32)
        result[at, pl.ds(3 * width, width)] = (d * normed).astype(result.dtype)
        dn = d * u[at, :].astype(jnp.float32)
        mean_dn = jnp.mean(dn, axis=1, keepdims=True)
        mean_dnn = jnp.mean(dn * normed, axis=1, keepdims=True)
        gm[at, :] = (rstd * (dn - mean_dn - normed * mean_dnn)).astype(gm.dtype)

    written = set()
    left = {}
    for e in range((MAXLEN + rows) // CHUNK):
        users = [b for b in range(blocks) if b * BLOCK <= e * CHUNK < b * BLOCK + KEYS]
        for c in range(quads):
            left[e, c] = len(users)

    def add(b, c, part, value):
        for i in range(KEYS // CHUNK):
            e = b * BLOCK // CHUNK + i
            piece = value[i * CHUNK : (i + 1) * CHUNK]
            at = pl.ds(e * CHUNK, CHUNK)
            if (e, c, part) in written:
                piece = piece + acc[at, columns(c, part)]
            written.add((e, c, part))
            if part:
                left[e, c] -= 1
            remaining = left[e, c] if part else left[e, c] - 1
            row = e * CHUNK - MAXLEN
            if remaining or row >= tail:
                acc[at, columns(c, part)] = piece
            elif row < 0:
                outgoing[c, at, pl.ds(part * quad, quad)] = piece.astype(outgoing.dtype)
            else:
                result[pl.ds(row, CHUNK), columns(c, 1 + part)] = piece.astype(result.dtype)

    def backward(b, c):
        keys = kv[pl.ds(b * BLOCK, KEYS), columns(c)]
        values = kv[pl.ds(b * BLOCK, KEYS), columns(c, 1)]
        queries = stacked(q[block_rows(b), columns(c)], sixteenths)
        grads = stacked(gm[block_rows(b), columns(c)], ones)
        grad_weights = dot(values, grads, 1, 1)
        grad_scores = (grad_weights * slopes[b, c]).astype(jnp.bfloat16)
        add(b, c, 0, dot(grad_scores, queries, 1, 0))
        add(b, c, 1, dot(weights[b, c], grads, 1, 0))
        grad_q = per_head(grad_scores, keys) * 0.0625
        result[block_rows(b), columns(c)] = grad_q.astype(result.dtype)

    stores = []

    def store(row, height, column, span):
        at = (pl.ds(row, height), pl.ds(column, span))
        copy = pltpu.make_async_copy(result.at[at], out.at[at], store_sem.at[len(stores)])
        copy.start()
        stores.append(copy)

    lower, upper = range(half), range(half, blocks)
    split = half * BLOCK

    for copy in loads[:2]:
        copy.wait()
    for c in range(quads):
        for b in upper:
            forward(b, c)
    for copy in loads[2:]:
        copy.wait()
    for b in upper:
        normalise(b)
    store(split, rows - split, 3 * width, width)

    @pl.when(has_prev)
    def _():
        halo.wait_recv()

    for c in range(quads):
        for b in lower:
            forward(b, c)
    for b in lower:
        normalise(b)
    store(0, split, 3 * width, width)
    for c in range(quads):
        for b in lower:
            backward(b, c)

        @pl.when(has_prev)
        def _():
            backs(c).start()

    store(0, split, 0, width)
    for c in range(quads):
        for b in upper:
            backward(b, c)
    store(split, rows - split, 0, width)
    store(0, tail, width, 2 * width)

    for c in range(quads):

        @pl.when(has_next)
        def _():
            backs(c).wait_recv()

        for part in range(2):
            total = acc[pl.ds(rows, MAXLEN), columns(c, part)] + returned[
                c, :, pl.ds(part * quad, quad)
            ].astype(jnp.float32)
            result[pl.ds(tail, MAXLEN), columns(c, 1 + part)] = total.astype(result.dtype)
    store(tail, MAXLEN, width, 2 * width)

    @pl.when(has_next)
    def _():
        halo.wait_send()

    for c in range(quads):

        @pl.when(has_prev)
        def _():
            backs(c).wait_send()

    for copy in stores:
        copy.wait()


def on_device(mesh, projected, grad_gated, lengths):
    rows, width = grad_gated.shape
    quad = QUAD * (width // HEADS)
    quads = width // quad
    blocks = rows // BLOCK
    bf16, f32 = jnp.bfloat16, jnp.float32
    window = rows + MAXLEN
    anywhere = pl.BlockSpec(memory_space=pl.ANY)
    return pl.pallas_call(
        functools.partial(kernel, mesh.shape["dp"], mesh.shape["shard"]),
        out_shape=jax.ShapeDtypeStruct((rows, 4 * width), bf16),
        in_specs=[anywhere, anywhere, pl.BlockSpec(memory_space=pltpu.VMEM)],
        out_specs=anywhere,
        scratch_shapes=[
            pltpu.VMEM((window, 2 * width), bf16),
            pltpu.VMEM((rows, width), bf16),
            pltpu.VMEM((rows, width), bf16),
            pltpu.VMEM((rows, width), bf16),
            pltpu.VMEM((rows, width), f32),
            pltpu.VMEM((rows, width), bf16),
            pltpu.VMEM((blocks, quads, KEYS, quad), bf16),
            pltpu.VMEM((blocks, quads, KEYS, quad), f32),
            pltpu.VMEM((window, 2 * width), f32),
            pltpu.VMEM((quad, quad), bf16),
            pltpu.VMEM((quad, quad), bf16),
            pltpu.VMEM((blocks, KEYS, quad), f32),
            pltpu.VMEM((rows, 4 * width), bf16),
            pltpu.VMEM((quads, MAXLEN, 2 * quad), bf16),
            pltpu.VMEM((quads, MAXLEN, 2 * quad), bf16),
            pltpu.SemaphoreType.DMA((4,)),
            pltpu.SemaphoreType.DMA((6,)),
            pltpu.SemaphoreType.DMA,
            pltpu.SemaphoreType.DMA,
            pltpu.SemaphoreType.DMA((quads,)),
            pltpu.SemaphoreType.DMA((quads,)),
        ],
        compiler_params=pltpu.CompilerParams(
            collective_id=0, has_side_effects=True, vmem_limit_bytes=40 * 1024 * 1024
        ),
        cost_estimate=pl.CostEstimate(
            flops=6 * 2 * rows * KEYS * width * QUAD,
            bytes_accessed=rows * width * 2 * 9,
            transcendentals=rows * KEYS * HEADS,
        ),
    )(projected, grad_gated, lengths.reshape(1, -1))


def solution(mesh):
    in_specs = (P(("groups", "dp", "shard"), None), P(("groups", "dp", "shard"), None), P("groups"))
    out_specs = P(("groups", "dp", "shard"), None)
    return jax.shard_map(
        functools.partial(on_device, mesh),
        mesh=mesh, in_specs=in_specs, out_specs=out_specs, check_vma=False,
    )
```

```python
import functools

import jax
import jax.numpy as jnp
from jax import lax
from jax.experimental import pallas as pl
from jax.experimental.pallas import tpu as pltpu
from jax.sharding import PartitionSpec as P

HEADS = 16
MAXLEN = 96
BLOCK = 64
KEYS = BLOCK + MAXLEN
QUAD = 4
CHUNK = 32
MESH = pl.DeviceIdType.MESH


def dot(a, b, ca, cb):
    return lax.dot_general(a, b, (((ca,), (cb,)), ((), ())), preferred_element_type=jnp.float32)


def kernel(
    n_dp, n_shard,
    proj, grad, counts, result,
    lengths, kv, q, u, dy, mixed, gm, weights, slopes, acc, ones, sixteenths, masks,
    outgoing, returned,
    load_sem, halo_send, halo_recv, back_send, back_recv,
):
    rows, width = q.shape
    quad = QUAD * (width // HEADS)
    quads = width // quad
    blocks = rows // BLOCK
    tail = rows - MAXLEN
    half = blocks // 2

    me = lax.axis_index("dp") * n_shard + lax.axis_index("shard")
    last = n_dp * n_shard - 1
    has_prev, has_next = me > 0, me < last

    def columns(c, part=0):
        return pl.ds(part * width + c * quad, quad)

    def device(index):
        return {"dp": index // n_shard, "shard": index % n_shard}

    barrier = pltpu.get_barrier_semaphore()

    @pl.when(has_prev)
    def _():
        pl.semaphore_signal(barrier, inc=1, device_id=device(me - 1), device_id_type=MESH)

    @pl.when(has_next)
    def _():
        pl.semaphore_signal(barrier, inc=1, device_id=device(me + 1), device_id_type=MESH)

    def load(i, source, target):
        copy = pltpu.make_async_copy(source, target, load_sem.at[i])
        copy.start()
        return copy

    loads = [
        load(0, proj.at[:, pl.ds(width, 2 * width)], kv.at[pl.ds(MAXLEN, rows), :]),
        load(1, proj.at[:, pl.ds(0, width)], q),
        load(2, proj.at[:, pl.ds(3 * width, width)], u),
        load(3, grad, dy),
        load(4, counts, lengths),
    ]

    pl.semaphore_wait(barrier, jnp.where(has_prev, 1, 0) + jnp.where(has_next, 1, 0))

    def halo(c, part):
        return pltpu.make_async_remote_copy(
            src_ref=proj.at[pl.ds(tail, MAXLEN), columns(c, 1 + part)],
            dst_ref=kv.at[pl.ds(0, MAXLEN), columns(c, part)],
            send_sem=halo_send.at[c, part],
            recv_sem=halo_recv.at[c, part],
            device_id=device(jnp.where(has_next, me + 1, me - 1)),
            device_id_type=MESH,
        )

    halves = [(c, part) for c in range(quads) for part in range(2)]

    @pl.when(has_next)
    def _():
        for c, part in halves:
            halo(c, part).start()

    @pl.when(jnp.logical_not(has_prev))
    def _():
        kv[pl.ds(0, MAXLEN), :] = jnp.zeros((MAXLEN, 2 * width), kv.dtype)

    @pl.when(jnp.logical_not(has_next))
    def _():
        returned[...] = jnp.zeros_like(returned)

    def backs(c):
        return pltpu.make_async_remote_copy(
            src_ref=outgoing.at[c],
            dst_ref=returned.at[c],
            send_sem=back_send.at[c],
            recv_sem=back_recv.at[c],
            device_id=device(jnp.where(has_prev, me - 1, me + 1)),
            device_id_type=MESH,
        )

    loads[4].wait()

    base = (me * rows).astype(jnp.float32)
    lane = (lax.broadcasted_iota(jnp.int32, (1, quad), 1) % BLOCK).astype(jnp.float32)
    positions = [base + float(b * BLOCK) + lane for b in range(blocks)]
    starts = [jnp.zeros((1, quad), jnp.float32) for _ in range(blocks)]
    carry = jnp.zeros((1, 1), jnp.float32)
    count = lengths.shape[1]
    for first in range(0, count, 128):
        span = min(128, count - first)
        part = lengths[:, first : first + span].astype(jnp.float32)
        upto = lax.broadcasted_iota(jnp.int32, (span, span), 1) <= lax.broadcasted_iota(
            jnp.int32, (span, span), 0
        )
        ends = carry + jnp.sum(jnp.where(upto, part, 0.0), axis=1, keepdims=True)
        carry = carry + jnp.sum(part, axis=1, keepdims=True)
        for b in range(blocks):
            reached = jnp.max(jnp.where(ends <= positions[b], ends, 0.0), axis=0, keepdims=True)
            starts[b] = jnp.maximum(starts[b], reached)
    offset = lax.broadcasted_iota(jnp.int32, (KEYS, quad), 0).astype(jnp.float32)
    for b in range(blocks):
        key = offset + (base + float(b * BLOCK - MAXLEN))
        keep = (starts[b] <= key) & (key <= positions[b])
        masks[b] = jnp.where(keep, 1.0, 0.0)

    own_head = (
        lax.broadcasted_iota(jnp.int32, (quad, quad), 0) // BLOCK
        == lax.broadcasted_iota(jnp.int32, (quad, quad), 1) // (quad // QUAD)
    )
    ones[...] = jnp.where(own_head, 1.0, 0.0).astype(ones.dtype)
    sixteenths[...] = jnp.where(own_head, 0.0625, 0.0).astype(ones.dtype)
    left_head = lax.broadcasted_iota(jnp.int32, (BLOCK, quad // 2), 1) < quad // QUAD

    def stacked(value, head_mask):
        return jnp.concatenate([value] * QUAD, 0) * head_mask[...]

    def block_rows(b):
        return pl.ds(b * BLOCK, BLOCK)

    def per_head(transposed, values):
        halves = []
        for p in range(2):
            lanes = slice(p * quad // 2, (p + 1) * quad // 2)
            both = dot(transposed[:, lanes], values[:, lanes], 0, 0)
            halves.append(jnp.where(left_head, both[:BLOCK], both[BLOCK:]))
        return jnp.concatenate(halves, 1)

    def forward(b, c):
        keys = kv[pl.ds(b * BLOCK, KEYS), columns(c)]
        values = kv[pl.ds(b * BLOCK, KEYS), columns(c, 1)]
        queries = stacked(q[block_rows(b), columns(c)], sixteenths)
        h = dot(keys, queries, 1, 1)
        t = jnp.tanh(h)
        kept = (1.0 + t) * masks[b]
        w = (h * kept).astype(weights.dtype)
        weights[b, c] = w
        slopes[b, c] = kept * (1.0 + h * (1.0 - t))
        mixed[block_rows(b), columns(c)] = per_head(w, values)

    def normalise(b):
        at = block_rows(b)
        m = mixed[at, :]
        centered = m - jnp.mean(m, axis=1, keepdims=True)
        rstd = lax.rsqrt(jnp.mean(centered * centered, axis=1, keepdims=True) + 1e-05)
        normed = centered * rstd
        d = dy[at, :].astype(jnp.float32)
        result[at, pl.ds(3 * width, width)] = (d * normed).astype(result.dtype)
        dn = d * u[at, :].astype(jnp.float32)
        mean_dn = jnp.mean(dn, axis=1, keepdims=True)
        mean_dnn = jnp.mean(dn * normed, axis=1, keepdims=True)
        gm[at, :] = (rstd * (dn - mean_dn - normed * mean_dnn)).astype(gm.dtype)

    written = set()
    left = {}
    for e in range((MAXLEN + rows) // CHUNK):
        users = [b for b in range(blocks) if b * BLOCK <= e * CHUNK < b * BLOCK + KEYS]
        for c in range(quads):
            left[e, c] = len(users)

    def add(b, c, part, value):
        for i in range(KEYS // CHUNK):
            e = b * BLOCK // CHUNK + i
            piece = value[i * CHUNK : (i + 1) * CHUNK]
            at = pl.ds(e * CHUNK, CHUNK)
            if (e, c, part) in written:
                piece = piece + acc[at, columns(c, part)]
            written.add((e, c, part))
            if part:
                left[e, c] -= 1
            remaining = left[e, c] if part else left[e, c] - 1
            row = e * CHUNK - MAXLEN
            if remaining or row >= tail:
                acc[at, columns(c, part)] = piece
            elif row < 0:
                outgoing[c, at, pl.ds(part * quad, quad)] = piece.astype(outgoing.dtype)
            else:
                result[pl.ds(row, CHUNK), columns(c, 1 + part)] = piece.astype(result.dtype)

    def backward(b, c):
        keys = kv[pl.ds(b * BLOCK, KEYS), columns(c)]
        values = kv[pl.ds(b * BLOCK, KEYS), columns(c, 1)]
        queries = stacked(q[block_rows(b), columns(c)], sixteenths)
        grads = stacked(gm[block_rows(b), columns(c)], ones)
        grad_weights = dot(values, grads, 1, 1)
        grad_scores = (grad_weights * slopes[b, c]).astype(jnp.bfloat16)
        add(b, c, 0, dot(grad_scores, queries, 1, 0))
        add(b, c, 1, dot(weights[b, c], grads, 1, 0))
        grad_q = per_head(grad_scores, keys) * 0.0625
        result[block_rows(b), columns(c)] = grad_q.astype(result.dtype)

    lower, upper = range(blocks // 2), range(blocks // 2, blocks)

    for copy in loads[:2]:
        copy.wait()
    for c in range(quads):
        for b in upper:
            forward(b, c)
    for copy in loads[2:4]:
        copy.wait()
    for b in upper:
        normalise(b)
    for c in range(quads):
        for b in upper:
            backward(b, c)

    for c in range(quads):

        @pl.when(has_prev)
        def _():
            halo(c, 0).wait_recv()
            halo(c, 1).wait_recv()

        for b in lower:
            forward(b, c)
    for b in lower:
        normalise(b)
    for c in range(quads):
        for b in lower:
            backward(b, c)

        @pl.when(has_prev)
        def _():
            backs(c).start()

    for c in range(quads):

        @pl.when(has_next)
        def _():
            backs(c).wait_recv()

        for part in range(2):
            total = acc[pl.ds(rows, MAXLEN), columns(c, part)] + returned[
                c, :, pl.ds(part * quad, quad)
            ].astype(jnp.float32)
            result[pl.ds(tail, MAXLEN), columns(c, 1 + part)] = total.astype(result.dtype)

    @pl.when(has_next)
    def _():
        for c, part in halves:
            halo(c, part).wait_send()

    @pl.when(has_prev)
    def _():
        for c in range(quads):
            backs(c).wait_send()


def on_device(mesh, projected, grad_gated, lengths):
    rows, width = grad_gated.shape
    quad = QUAD * (width // HEADS)
    quads = width // quad
    blocks = rows // BLOCK
    bf16, f32 = jnp.bfloat16, jnp.float32
    window = rows + MAXLEN
    hbm = pl.BlockSpec(memory_space=pltpu.HBM)
    counts = lengths.reshape(1, -1)
    return pl.pallas_call(
        functools.partial(kernel, mesh.shape["dp"], mesh.shape["shard"]),
        out_shape=jax.ShapeDtypeStruct((rows, 4 * width), bf16),
        in_specs=[hbm, hbm, hbm],
        out_specs=pl.BlockSpec(memory_space=pltpu.VMEM),
        scratch_shapes=[
            pltpu.VMEM(counts.shape, jnp.int32),
            pltpu.VMEM((window, 2 * width), bf16),
            pltpu.VMEM((rows, width), bf16),
            pltpu.VMEM((rows, width), bf16),
            pltpu.VMEM((rows, width), bf16),
            pltpu.VMEM((rows, width), f32),
            pltpu.VMEM((rows, width), bf16),
            pltpu.VMEM((blocks, quads, KEYS, quad), bf16),
            pltpu.VMEM((blocks, quads, KEYS, quad), f32),
            pltpu.VMEM((window, 2 * width), f32),
            pltpu.VMEM((quad, quad), bf16),
            pltpu.VMEM((quad, quad), bf16),
            pltpu.VMEM((blocks, KEYS, quad), f32),
            pltpu.VMEM((quads, MAXLEN, 2 * quad), bf16),
            pltpu.VMEM((quads, MAXLEN, 2 * quad), bf16),
            pltpu.SemaphoreType.DMA((5,)),
            pltpu.SemaphoreType.DMA((quads, 2)),
            pltpu.SemaphoreType.DMA((quads, 2)),
            pltpu.SemaphoreType.DMA((quads,)),
            pltpu.SemaphoreType.DMA((quads,)),
        ],
        compiler_params=pltpu.CompilerParams(
            collective_id=0, has_side_effects=True, vmem_limit_bytes=40 * 1024 * 1024
        ),
        cost_estimate=pl.CostEstimate(
            flops=6 * 2 * rows * KEYS * width * QUAD,
            bytes_accessed=rows * width * 2 * 9,
            transcendentals=rows * KEYS * HEADS,
        ),
    )(*(pltpu.with_memory_space_constraint(a, pltpu.HBM) for a in (projected, grad_gated, counts)))


def solution(mesh):
    in_specs = (P(("groups", "dp", "shard"), None), P(("groups", "dp", "shard"), None), P("groups"))
    out_specs = P(("groups", "dp", "shard"), None)
    return jax.shard_map(
        functools.partial(on_device, mesh),
        mesh=mesh, in_specs=in_specs, out_specs=out_specs, check_vma=False,
    )
```

```python
import functools

import jax
import jax.numpy as jnp
from jax import lax
from jax.experimental import pallas as pl
from jax.experimental.pallas import tpu as pltpu
from jax.sharding import PartitionSpec as P

HEADS = 16
MAXLEN = 96
BLOCK = 64
KEYS = BLOCK + MAXLEN
QUAD = 4
CHUNK = 32
MESH = pl.DeviceIdType.MESH


def dot(a, b, ca, cb):
    return lax.dot_general(a, b, (((ca,), (cb,)), ((), ())), preferred_element_type=jnp.float32)


def kernel(
    n_dp, n_shard,
    proj, grad, counts, result,
    lengths, kv, q, u, dy, mixed, gm, weights, slopes, acc, ones, sixteenths, masks,
    load_sem, halo_send, halo_recv, back_send, back_recv,
):
    rows, width = dy.shape
    quad = QUAD * (width // HEADS)
    quads = width // quad
    blocks = rows // BLOCK
    tail = rows - MAXLEN
    every = q.shape[0] // BLOCK

    me = lax.axis_index("dp") * n_shard + lax.axis_index("shard")
    last = n_dp * n_shard - 1
    has_prev, has_next = me > 0, me < last

    def columns(c, part=0):
        return pl.ds(part * width + c * quad, quad)

    def device(index):
        return {"dp": index // n_shard, "shard": index % n_shard}

    barrier = pltpu.get_barrier_semaphore()

    @pl.when(has_prev)
    def _():
        pl.semaphore_signal(barrier, inc=1, device_id=device(me - 1), device_id_type=MESH)

    @pl.when(has_next)
    def _():
        pl.semaphore_signal(barrier, inc=1, device_id=device(me + 1), device_id_type=MESH)

    def load(i, source, target):
        copy = pltpu.make_async_copy(source, target, load_sem.at[i])
        copy.start()
        return copy

    loads = [
        load(0, proj.at[:, pl.ds(width, 2 * width)], kv.at[pl.ds(MAXLEN, rows), :]),
        load(1, proj.at[:, pl.ds(0, width)], q.at[pl.ds(0, rows), :]),
        load(2, proj.at[:, pl.ds(3 * width, width)], u),
        load(3, grad, dy),
        load(4, counts, lengths),
    ]

    pl.semaphore_wait(barrier, jnp.where(has_prev, 1, 0) + jnp.where(has_next, 1, 0))

    def halo(c, part):
        return pltpu.make_async_remote_copy(
            src_ref=proj.at[pl.ds(tail, MAXLEN), columns(c, 1 + part)],
            dst_ref=kv.at[pl.ds(0, MAXLEN), columns(c, part)],
            send_sem=halo_send.at[c, part],
            recv_sem=halo_recv.at[c, part],
            device_id=device(jnp.where(has_next, me + 1, me - 1)),
            device_id_type=MESH,
        )

    halves = [(c, part) for c in range(quads) for part in range(2)]

    @pl.when(has_next)
    def _():
        for c, part in halves:
            halo(c, part).start()

    @pl.when(jnp.logical_not(has_prev))
    def _():
        kv[pl.ds(0, MAXLEN), :] = jnp.zeros((MAXLEN, 2 * width), kv.dtype)

    @pl.when(jnp.logical_not(has_next))
    def _():
        for ref in (q, gm):
            ref[pl.ds(rows, MAXLEN), :] = jnp.zeros((MAXLEN, width), ref.dtype)

    beyond = q.shape[0] - rows - MAXLEN
    for ref in (q, gm):
        ref[pl.ds(rows + MAXLEN, beyond), :] = jnp.zeros((beyond, width), ref.dtype)

    def to_prev(i, source, target):
        return pltpu.make_async_remote_copy(
            src_ref=source,
            dst_ref=target,
            send_sem=back_send.at[i],
            recv_sem=back_recv.at[i],
            device_id=device(jnp.where(has_prev, me - 1, me + 1)),
            device_id_type=MESH,
        )

    def gm_part(i, row, height):
        return to_prev(i, gm.at[pl.ds(row, height), :], gm.at[pl.ds(rows + row, height), :])

    backs = [
        to_prev(0, proj.at[pl.ds(0, MAXLEN), pl.ds(0, width)], q.at[pl.ds(rows, MAXLEN), :]),
        gm_part(1, 0, BLOCK),
        gm_part(2, BLOCK, MAXLEN - BLOCK),
    ]

    loads[4].wait()

    base = (me * rows).astype(jnp.float32)
    lane = (lax.broadcasted_iota(jnp.int32, (1, quad), 1) % BLOCK).astype(jnp.float32)
    positions = [base + float(b * BLOCK) + lane for b in range(every)]
    starts = [jnp.zeros((1, quad), jnp.float32) for _ in range(every)]
    carry = jnp.zeros((1, 1), jnp.float32)
    count = lengths.shape[1]
    for first in range(0, count, 128):
        span = min(128, count - first)
        part = lengths[:, first : first + span].astype(jnp.float32)
        upto = lax.broadcasted_iota(jnp.int32, (span, span), 1) <= lax.broadcasted_iota(
            jnp.int32, (span, span), 0
        )
        ends = carry + jnp.sum(jnp.where(upto, part, 0.0), axis=1, keepdims=True)
        carry = carry + jnp.sum(part, axis=1, keepdims=True)
        for b in range(every):
            reached = jnp.max(jnp.where(ends <= positions[b], ends, 0.0), axis=0, keepdims=True)
            starts[b] = jnp.maximum(starts[b], reached)
    offset = lax.broadcasted_iota(jnp.int32, (KEYS, quad), 0).astype(jnp.float32)
    for b in range(every):
        key = offset + (base + float(b * BLOCK - MAXLEN))
        keep = (starts[b] <= key) & (key <= positions[b])
        masks[b] = jnp.where(keep, 1.0, 0.0)

    own_head = (
        lax.broadcasted_iota(jnp.int32, (quad, quad), 0) // BLOCK
        == lax.broadcasted_iota(jnp.int32, (quad, quad), 1) // (quad // QUAD)
    )
    ones[...] = jnp.where(own_head, 1.0, 0.0).astype(ones.dtype)
    sixteenths[...] = jnp.where(own_head, 0.0625, 0.0).astype(ones.dtype)
    left_head = lax.broadcasted_iota(jnp.int32, (BLOCK, quad // 2), 1) < quad // QUAD

    def stacked(value, head_mask):
        return jnp.concatenate([value] * QUAD, 0) * head_mask[...]

    def block_rows(b):
        return pl.ds(b * BLOCK, BLOCK)

    def per_head(transposed, values):
        halves = []
        for p in range(2):
            lanes = slice(p * quad // 2, (p + 1) * quad // 2)
            both = dot(transposed[:, lanes], values[:, lanes], 0, 0)
            halves.append(jnp.where(left_head, both[:BLOCK], both[BLOCK:]))
        return jnp.concatenate(halves, 1)

    def reach(b):
        return min(KEYS, MAXLEN + rows - b * BLOCK)

    def forward(b, c):
        span = reach(b)
        keys = kv[pl.ds(b * BLOCK, span), columns(c)]
        queries = stacked(q[block_rows(b), columns(c)], sixteenths)
        h = dot(keys, queries, 1, 1)
        t = jnp.tanh(h)
        kept = (1.0 + t) * masks[b, pl.ds(0, span), :]
        w = (h * kept).astype(weights.dtype)
        weights[b, c, pl.ds(0, span), :] = w
        slopes[b, c, pl.ds(0, span), :] = kept * (1.0 + h * (1.0 - t))
        if b < blocks:
            values = kv[pl.ds(b * BLOCK, span), columns(c, 1)]
            mixed[block_rows(b), columns(c)] = per_head(w, values)

    def normalise(b):
        at = block_rows(b)
        m = mixed[at, :]
        centered = m - jnp.mean(m, axis=1, keepdims=True)
        rstd = lax.rsqrt(jnp.mean(centered * centered, axis=1, keepdims=True) + 1e-05)
        normed = centered * rstd
        d = dy[at, :].astype(jnp.float32)
        result[at, pl.ds(3 * width, width)] = (d * normed).astype(result.dtype)
        dn = d * u[at, :].astype(jnp.float32)
        mean_dn = jnp.mean(dn, axis=1, keepdims=True)
        mean_dnn = jnp.mean(dn * normed, axis=1, keepdims=True)
        gm[at, :] = (rstd * (dn - mean_dn - normed * mean_dnn)).astype(gm.dtype)

    written = set()
    left = {}
    for e in range(MAXLEN // CHUNK, (MAXLEN + rows) // CHUNK):
        users = [b for b in range(every) if b * BLOCK <= e * CHUNK < b * BLOCK + KEYS]
        for c in range(quads):
            for part in range(2):
                left[e, c, part] = len(users)

    def add(b, c, part, row, value):
        for i in range(value.shape[0] // CHUNK):
            key = (row // CHUNK + i, c, part)
            piece = value[i * CHUNK : (i + 1) * CHUNK]
            at = pl.ds(row + i * CHUNK, CHUNK)
            if key in written:
                piece = piece + acc[at, columns(c, part)]
            written.add(key)
            left[key] -= 1
            if left[key]:
                acc[at, columns(c, part)] = piece
            else:
                own = pl.ds(row + i * CHUNK - MAXLEN, CHUNK)
                result[own, columns(c, 1 + part)] = piece.astype(result.dtype)

    def backward(b, c):
        span = reach(b)
        skip = max(0, MAXLEN - b * BLOCK)
        keys = kv[pl.ds(b * BLOCK, span), columns(c)]
        values = kv[pl.ds(b * BLOCK, span), columns(c, 1)]
        queries = stacked(q[block_rows(b), columns(c)], sixteenths)
        grads = stacked(gm[block_rows(b), columns(c)], ones)
        grad_weights = dot(values, grads, 1, 1)
        grad_scores = (grad_weights * slopes[b, c, pl.ds(0, span), :]).astype(jnp.bfloat16)
        add(b, c, 0, b * BLOCK + skip, dot(grad_scores[skip:], queries, 1, 0))
        w = weights[b, c, pl.ds(skip, span - skip), :]
        add(b, c, 1, b * BLOCK + skip, dot(w, grads, 1, 0))
        if b < blocks:
            grad_q = per_head(grad_scores, keys) * 0.0625
            result[block_rows(b), columns(c)] = grad_q.astype(result.dtype)

    lower, upper = range(blocks // 2), range(blocks // 2, blocks)
    after = range(blocks, every)

    for copy in loads[:2]:
        copy.wait()
    for c in range(quads):
        for b in upper:
            forward(b, c)
    for copy in loads[2:4]:
        copy.wait()
    for b in upper:
        normalise(b)
    for c in range(quads):
        for b in upper:
            backward(b, c)

    @pl.when(has_prev)
    def _():
        backs[0].start()

    for c in range(quads):

        @pl.when(has_prev)
        def _():
            halo(c, 0).wait_recv()
            halo(c, 1).wait_recv()

        for b in lower:
            forward(b, c)
    for b in lower:
        normalise(b)

        @pl.when(has_prev)
        def _():
            backs[1 + b].start()

    for c in range(quads):
        for b in lower:
            backward(b, c)

    @pl.when(has_next)
    def _():
        backs[0].wait_recv()

    for c in range(quads):
        for b in after:
            forward(b, c)

    @pl.when(has_next)
    def _():
        backs[1].wait_recv()
        backs[2].wait_recv()

    for c in range(quads):
        for b in after:
            backward(b, c)

    @pl.when(has_next)
    def _():
        for c, part in halves:
            halo(c, part).wait_send()

    @pl.when(has_prev)
    def _():
        for back in backs:
            back.wait_send()


def on_device(mesh, projected, grad_gated, lengths):
    rows, width = grad_gated.shape
    quad = QUAD * (width // HEADS)
    quads = width // quad
    blocks = rows // BLOCK + 2
    bf16, f32 = jnp.bfloat16, jnp.float32
    window = rows + MAXLEN
    hbm = pl.BlockSpec(memory_space=pltpu.HBM)
    counts = lengths.reshape(1, -1)
    return pl.pallas_call(
        functools.partial(kernel, mesh.shape["dp"], mesh.shape["shard"]),
        out_shape=jax.ShapeDtypeStruct((rows, 4 * width), bf16),
        in_specs=[hbm, hbm, hbm],
        out_specs=pl.BlockSpec(memory_space=pltpu.VMEM),
        scratch_shapes=[
            pltpu.VMEM(counts.shape, jnp.int32),
            pltpu.VMEM((window, 2 * width), bf16),
            pltpu.VMEM((blocks * BLOCK, width), bf16),
            pltpu.VMEM((rows, width), bf16),
            pltpu.VMEM((rows, width), bf16),
            pltpu.VMEM((rows, width), f32),
            pltpu.VMEM((blocks * BLOCK, width), bf16),
            pltpu.VMEM((blocks, quads, KEYS, quad), bf16),
            pltpu.VMEM((blocks, quads, KEYS, quad), f32),
            pltpu.VMEM((window, 2 * width), f32),
            pltpu.VMEM((quad, quad), bf16),
            pltpu.VMEM((quad, quad), bf16),
            pltpu.VMEM((blocks, KEYS, quad), f32),
            pltpu.SemaphoreType.DMA((5,)),
            pltpu.SemaphoreType.DMA((quads, 2)),
            pltpu.SemaphoreType.DMA((quads, 2)),
            pltpu.SemaphoreType.DMA((3,)),
            pltpu.SemaphoreType.DMA((3,)),
        ],
        compiler_params=pltpu.CompilerParams(
            collective_id=0, has_side_effects=True, vmem_limit_bytes=40 * 1024 * 1024
        ),
        cost_estimate=pl.CostEstimate(
            flops=6 * 2 * rows * KEYS * width * QUAD,
            bytes_accessed=rows * width * 2 * 9,
            transcendentals=rows * KEYS * HEADS,
        ),
    )(*(pltpu.with_memory_space_constraint(a, pltpu.HBM) for a in (projected, grad_gated, counts)))


def solution(mesh):
    in_specs = (P(("groups", "dp", "shard"), None), P(("groups", "dp", "shard"), None), P("groups"))
    out_specs = P(("groups", "dp", "shard"), None)
    return jax.shard_map(
        functools.partial(on_device, mesh),
        mesh=mesh, in_specs=in_specs, out_specs=out_specs, check_vma=False,
    )
```

```python
import functools

import jax
import jax.numpy as jnp
from jax import lax
from jax.experimental import pallas as pl
from jax.experimental.pallas import tpu as pltpu
from jax.sharding import PartitionSpec as P

HEADS = 16
MAXLEN = 96
BLOCK = 64
KEYS = BLOCK + MAXLEN
QUAD = 4
CHUNK = 32
MESH = pl.DeviceIdType.MESH


def dot(a, b, ca, cb):
    return lax.dot_general(a, b, (((ca,), (cb,)), ((), ())), preferred_element_type=jnp.float32)


def kernel(
    n_dp, n_shard,
    proj, grad, counts, result,
    lengths, kv, q, u, dy, mixed, gm, weights, slopes, acc, ones, sixteenths, masks,
    load_sem, halo_send, halo_recv, back_send, back_recv,
):
    rows, width = dy.shape
    quad = QUAD * (width // HEADS)
    quads = width // quad
    blocks = rows // BLOCK
    tail = rows - MAXLEN
    every = q.shape[0] // BLOCK

    me = lax.axis_index("dp") * n_shard + lax.axis_index("shard")
    last = n_dp * n_shard - 1
    has_prev, has_next = me > 0, me < last

    def columns(c, part=0):
        return pl.ds(part * width + c * quad, quad)

    def device(index):
        return {"dp": index // n_shard, "shard": index % n_shard}

    barrier = pltpu.get_barrier_semaphore()

    @pl.when(has_prev)
    def _():
        pl.semaphore_signal(barrier, inc=1, device_id=device(me - 1), device_id_type=MESH)

    @pl.when(has_next)
    def _():
        pl.semaphore_signal(barrier, inc=1, device_id=device(me + 1), device_id_type=MESH)

    def load(i, source, target):
        copy = pltpu.make_async_copy(source, target, load_sem.at[i])
        copy.start()
        return copy

    loads = [
        load(0, proj.at[:, pl.ds(width, 2 * width)], kv.at[pl.ds(MAXLEN, rows), :]),
        load(1, proj.at[:, pl.ds(0, width)], q.at[pl.ds(0, rows), :]),
        load(2, proj.at[:, pl.ds(3 * width, width)], u),
        load(3, grad, dy),
        load(4, counts, lengths),
    ]

    pl.semaphore_wait(barrier, jnp.where(has_prev, 1, 0) + jnp.where(has_next, 1, 0))

    def halo(i, row, height, column, span):
        return pltpu.make_async_remote_copy(
            src_ref=proj.at[pl.ds(tail + row, height), pl.ds(width + column, span)],
            dst_ref=kv.at[pl.ds(row, height), pl.ds(column, span)],
            send_sem=halo_send.at[i],
            recv_sem=halo_recv.at[i],
            device_id=device(jnp.where(has_next, me + 1, me - 1)),
            device_id_type=MESH,
        )

    near = halo(0, BLOCK, MAXLEN - BLOCK, 0, 2 * width)
    far = [
        [halo(1 + 2 * c + part, 0, BLOCK, part * width + c * quad, quad) for part in range(2)]
        for c in range(quads)
    ]
    halos = [near] + sum(far, [])

    @pl.when(has_next)
    def _():
        for copy in halos:
            copy.start()

    @pl.when(jnp.logical_not(has_prev))
    def _():
        kv[pl.ds(0, MAXLEN), :] = jnp.zeros((MAXLEN, 2 * width), kv.dtype)

    @pl.when(jnp.logical_not(has_next))
    def _():
        for ref in (q, gm):
            ref[pl.ds(rows, MAXLEN), :] = jnp.zeros((MAXLEN, width), ref.dtype)

    beyond = q.shape[0] - rows - MAXLEN
    for ref in (q, gm):
        ref[pl.ds(rows + MAXLEN, beyond), :] = jnp.zeros((beyond, width), ref.dtype)

    def to_prev(i, source, target):
        return pltpu.make_async_remote_copy(
            src_ref=source,
            dst_ref=target,
            send_sem=back_send.at[i],
            recv_sem=back_recv.at[i],
            device_id=device(jnp.where(has_prev, me - 1, me + 1)),
            device_id_type=MESH,
        )

    def gm_part(i, row, height, column, span):
        lanes = pl.ds(column, span)
        return to_prev(
            i, gm.at[pl.ds(row, height), lanes], gm.at[pl.ds(rows + row, height), lanes]
        )

    back_q = to_prev(
        0, proj.at[pl.ds(0, MAXLEN), pl.ds(0, width)], q.at[pl.ds(rows, MAXLEN), :]
    )
    back_second = gm_part(1, BLOCK, MAXLEN - BLOCK, 0, width)
    back_first = [gm_part(2 + c, 0, BLOCK, c * quad, quad) for c in range(quads)]
    backs = [back_q, back_second] + back_first

    loads[4].wait()

    base = (me * rows).astype(jnp.float32)
    lane = (lax.broadcasted_iota(jnp.int32, (1, quad), 1) % BLOCK).astype(jnp.float32)
    positions = [base + float(b * BLOCK) + lane for b in range(every)]
    starts = [jnp.zeros((1, quad), jnp.float32) for _ in range(every)]
    carry = jnp.zeros((1, 1), jnp.float32)
    count = lengths.shape[1]
    for first in range(0, count, 128):
        span = min(128, count - first)
        part = lengths[:, first : first + span].astype(jnp.float32)
        upto = lax.broadcasted_iota(jnp.int32, (span, span), 1) <= lax.broadcasted_iota(
            jnp.int32, (span, span), 0
        )
        ends = carry + jnp.sum(jnp.where(upto, part, 0.0), axis=1, keepdims=True)
        carry = carry + jnp.sum(part, axis=1, keepdims=True)
        for b in range(every):
            reached = jnp.max(jnp.where(ends <= positions[b], ends, 0.0), axis=0, keepdims=True)
            starts[b] = jnp.maximum(starts[b], reached)
    offset = lax.broadcasted_iota(jnp.int32, (KEYS, quad), 0).astype(jnp.float32)
    for b in range(every):
        key = offset + (base + float(b * BLOCK - MAXLEN))
        keep = (starts[b] <= key) & (key <= positions[b])
        masks[b] = jnp.where(keep, 1.0, 0.0)

    own_head = (
        lax.broadcasted_iota(jnp.int32, (quad, quad), 0) // BLOCK
        == lax.broadcasted_iota(jnp.int32, (quad, quad), 1) // (quad // QUAD)
    )
    ones[...] = jnp.where(own_head, 1.0, 0.0).astype(ones.dtype)
    sixteenths[...] = jnp.where(own_head, 0.0625, 0.0).astype(ones.dtype)
    left_head = lax.broadcasted_iota(jnp.int32, (BLOCK, quad // 2), 1) < quad // QUAD

    def stacked(value, head_mask):
        return jnp.concatenate([value] * QUAD, 0) * head_mask[...]

    def block_rows(b):
        return pl.ds(b * BLOCK, BLOCK)

    def per_head(transposed, values):
        halves = []
        for p in range(2):
            lanes = slice(p * quad // 2, (p + 1) * quad // 2)
            both = dot(transposed[:, lanes], values[:, lanes], 0, 0)
            halves.append(jnp.where(left_head, both[:BLOCK], both[BLOCK:]))
        return jnp.concatenate(halves, 1)

    def reach(b):
        return min(KEYS, MAXLEN + rows - b * BLOCK)

    def forward(b, c):
        span = reach(b)
        keys = kv[pl.ds(b * BLOCK, span), columns(c)]
        queries = stacked(q[block_rows(b), columns(c)], sixteenths)
        h = dot(keys, queries, 1, 1)
        t = jnp.tanh(h)
        kept = (1.0 + t) * masks[b, pl.ds(0, span), :]
        w = (h * kept).astype(weights.dtype)
        weights[b, c, pl.ds(0, span), :] = w
        slopes[b, c, pl.ds(0, span), :] = kept * (1.0 + h * (1.0 - t))
        if b < blocks:
            values = kv[pl.ds(b * BLOCK, span), columns(c, 1)]
            mixed[block_rows(b), columns(c)] = per_head(w, values)

    def normalise(b):
        at = block_rows(b)
        m = mixed[at, :]
        centered = m - jnp.mean(m, axis=1, keepdims=True)
        rstd = lax.rsqrt(jnp.mean(centered * centered, axis=1, keepdims=True) + 1e-05)
        normed = centered * rstd
        d = dy[at, :].astype(jnp.float32)
        result[at, pl.ds(3 * width, width)] = (d * normed).astype(result.dtype)
        dn = d * u[at, :].astype(jnp.float32)
        mean_dn = jnp.mean(dn, axis=1, keepdims=True)
        mean_dnn = jnp.mean(dn * normed, axis=1, keepdims=True)
        gm[at, :] = (rstd * (dn - mean_dn - normed * mean_dnn)).astype(gm.dtype)

    written = set()
    left = {}
    for e in range(MAXLEN // CHUNK, (MAXLEN + rows) // CHUNK):
        users = [b for b in range(every) if b * BLOCK <= e * CHUNK < b * BLOCK + KEYS]
        for c in range(quads):
            for part in range(2):
                left[e, c, part] = len(users)

    def add(b, c, part, row, value):
        for i in range(value.shape[0] // CHUNK):
            key = (row // CHUNK + i, c, part)
            piece = value[i * CHUNK : (i + 1) * CHUNK]
            at = pl.ds(row + i * CHUNK, CHUNK)
            if key in written:
                piece = piece + acc[at, columns(c, part)]
            written.add(key)
            left[key] -= 1
            if left[key]:
                acc[at, columns(c, part)] = piece
            else:
                own = pl.ds(row + i * CHUNK - MAXLEN, CHUNK)
                result[own, columns(c, 1 + part)] = piece.astype(result.dtype)

    def backward(b, c):
        span = reach(b)
        skip = max(0, MAXLEN - b * BLOCK)
        keys = kv[pl.ds(b * BLOCK, span), columns(c)]
        values = kv[pl.ds(b * BLOCK, span), columns(c, 1)]
        queries = stacked(q[block_rows(b), columns(c)], sixteenths)
        grads = stacked(gm[block_rows(b), columns(c)], ones)
        grad_weights = dot(values, grads, 1, 1)
        grad_scores = (grad_weights * slopes[b, c, pl.ds(0, span), :]).astype(jnp.bfloat16)
        add(b, c, 0, b * BLOCK + skip, dot(grad_scores[skip:], queries, 1, 0))
        w = weights[b, c, pl.ds(skip, span - skip), :]
        add(b, c, 1, b * BLOCK + skip, dot(w, grads, 1, 0))
        if b < blocks:
            grad_q = per_head(grad_scores, keys) * 0.0625
            result[block_rows(b), columns(c)] = grad_q.astype(result.dtype)

    upper, after = range(2, blocks), range(blocks, every)

    for copy in loads[:2]:
        copy.wait()
    for c in range(quads):
        for b in upper:
            forward(b, c)
    for copy in loads[2:4]:
        copy.wait()
    for b in upper:
        normalise(b)
    for c in range(quads):
        for b in upper:
            backward(b, c)

    @pl.when(has_prev)
    def _():
        back_q.start()
        near.wait_recv()

    for c in range(quads):
        forward(1, c)
    normalise(1)

    @pl.when(has_prev)
    def _():
        back_second.start()

    for c in range(quads):

        @pl.when(has_prev)
        def _():
            for copy in far[c]:
                copy.wait_recv()

        forward(0, c)
    normalise(0)

    @pl.when(has_prev)
    def _():
        for copy in back_first:
            copy.start()

    for b in (1, 0):
        for c in range(quads):
            backward(b, c)

    @pl.when(has_next)
    def _():
        back_q.wait_recv()

    for c in range(quads):
        for b in after:
            forward(b, c)

    @pl.when(has_next)
    def _():
        back_second.wait_recv()

    for c in range(quads):
        backward(blocks + 1, c)

    for c in range(quads):

        @pl.when(has_next)
        def _():
            back_first[c].wait_recv()

        backward(blocks, c)

    @pl.when(has_next)
    def _():
        for copy in halos:
            copy.wait_send()

    @pl.when(has_prev)
    def _():
        for copy in backs:
            copy.wait_send()


def on_device(mesh, projected, grad_gated, lengths):
    rows, width = grad_gated.shape
    quad = QUAD * (width // HEADS)
    quads = width // quad
    blocks = rows // BLOCK + 2
    bf16, f32 = jnp.bfloat16, jnp.float32
    window = rows + MAXLEN
    hbm = pl.BlockSpec(memory_space=pltpu.HBM)
    counts = lengths.reshape(1, -1)
    return pl.pallas_call(
        functools.partial(kernel, mesh.shape["dp"], mesh.shape["shard"]),
        out_shape=jax.ShapeDtypeStruct((rows, 4 * width), bf16),
        in_specs=[hbm, hbm, hbm],
        out_specs=pl.BlockSpec(memory_space=pltpu.VMEM),
        scratch_shapes=[
            pltpu.VMEM(counts.shape, jnp.int32),
            pltpu.VMEM((window, 2 * width), bf16),
            pltpu.VMEM((blocks * BLOCK, width), bf16),
            pltpu.VMEM((rows, width), bf16),
            pltpu.VMEM((rows, width), bf16),
            pltpu.VMEM((rows, width), f32),
            pltpu.VMEM((blocks * BLOCK, width), bf16),
            pltpu.VMEM((blocks, quads, KEYS, quad), bf16),
            pltpu.VMEM((blocks, quads, KEYS, quad), f32),
            pltpu.VMEM((window, 2 * width), f32),
            pltpu.VMEM((quad, quad), bf16),
            pltpu.VMEM((quad, quad), bf16),
            pltpu.VMEM((blocks, KEYS, quad), f32),
            pltpu.SemaphoreType.DMA((5,)),
            pltpu.SemaphoreType.DMA((1 + 2 * quads,)),
            pltpu.SemaphoreType.DMA((1 + 2 * quads,)),
            pltpu.SemaphoreType.DMA((2 + quads,)),
            pltpu.SemaphoreType.DMA((2 + quads,)),
        ],
        compiler_params=pltpu.CompilerParams(
            collective_id=0, has_side_effects=True, vmem_limit_bytes=40 * 1024 * 1024
        ),
        cost_estimate=pl.CostEstimate(
            flops=6 * 2 * rows * KEYS * width * QUAD,
            bytes_accessed=rows * width * 2 * 9,
            transcendentals=rows * KEYS * HEADS,
        ),
    )(*(pltpu.with_memory_space_constraint(a, pltpu.HBM) for a in (projected, grad_gated, counts)))


def solution(mesh):
    in_specs = (P(("groups", "dp", "shard"), None), P(("groups", "dp", "shard"), None), P("groups"))
    out_specs = P(("groups", "dp", "shard"), None)
    return jax.shard_map(
        functools.partial(on_device, mesh),
        mesh=mesh, in_specs=in_specs, out_specs=out_specs, check_vma=False,
    )
```

```python
import functools

import jax
import jax.numpy as jnp
from jax import lax
from jax.experimental import pallas as pl
from jax.experimental.pallas import tpu as pltpu
from jax.sharding import PartitionSpec as P

HEADS = 16
MAXLEN = 96
BLOCK = 64
KEYS = BLOCK + MAXLEN
QUAD = 4
PIECES = 2
CHUNK = 32
MESH = pl.DeviceIdType.MESH


def dot(a, b, ca, cb):
    return lax.dot_general(a, b, (((ca,), (cb,)), ((), ())), preferred_element_type=jnp.float32)


def kernel(
    n_dp, n_shard,
    proj, grad, counts, result,
    lengths, kv, q, u, dy, mixed, gm, weights, slopes, acc, ones, sixteenths, masks,
    load_sem, halo_send, halo_recv, back_send, back_recv,
):
    rows, width = dy.shape
    quad = QUAD * (width // HEADS)
    quads = width // quad
    piece_width = width // PIECES
    blocks = rows // BLOCK
    tail = rows - MAXLEN
    every = q.shape[0] // BLOCK

    me = lax.axis_index("dp") * n_shard + lax.axis_index("shard")
    last = n_dp * n_shard - 1
    has_prev, has_next = me > 0, me < last

    def columns(c, part=0):
        return pl.ds(part * width + c * quad, quad)

    def device(index):
        return {"dp": index // n_shard, "shard": index % n_shard}

    barrier = pltpu.get_barrier_semaphore()

    @pl.when(has_prev)
    def _():
        pl.semaphore_signal(barrier, inc=1, device_id=device(me - 1), device_id_type=MESH)

    @pl.when(has_next)
    def _():
        pl.semaphore_signal(barrier, inc=1, device_id=device(me + 1), device_id_type=MESH)

    def load(i, source, target):
        copy = pltpu.make_async_copy(source, target, load_sem.at[i])
        copy.start()
        return copy

    loads = [
        load(0, proj.at[:, pl.ds(width, 2 * width)], kv.at[pl.ds(MAXLEN, rows), :]),
        load(1, proj.at[:, pl.ds(0, width)], q.at[pl.ds(0, rows), :]),
        load(2, proj.at[:, pl.ds(3 * width, width)], u),
        load(3, grad, dy),
        load(4, counts, lengths),
    ]

    pl.semaphore_wait(barrier, jnp.where(has_prev, 1, 0) + jnp.where(has_next, 1, 0))

    def halo(i, row, height, column, span):
        return pltpu.make_async_remote_copy(
            src_ref=proj.at[pl.ds(tail + row, height), pl.ds(width + column, span)],
            dst_ref=kv.at[pl.ds(row, height), pl.ds(column, span)],
            send_sem=halo_send.at[i],
            recv_sem=halo_recv.at[i],
            device_id=device(jnp.where(has_next, me + 1, me - 1)),
            device_id_type=MESH,
        )

    near = halo(0, BLOCK, MAXLEN - BLOCK, 0, 2 * width)
    far = [
        [
            halo(1 + 2 * i + part, 0, BLOCK, part * width + i * piece_width, piece_width)
            for part in range(2)
        ]
        for i in range(PIECES)
    ]
    halos = [near] + sum(far, [])

    @pl.when(has_next)
    def _():
        for copy in halos:
            copy.start()

    @pl.when(jnp.logical_not(has_prev))
    def _():
        kv[pl.ds(0, MAXLEN), :] = jnp.zeros((MAXLEN, 2 * width), kv.dtype)

    @pl.when(jnp.logical_not(has_next))
    def _():
        for ref in (q, gm):
            ref[pl.ds(rows, MAXLEN), :] = jnp.zeros((MAXLEN, width), ref.dtype)

    beyond = q.shape[0] - rows - MAXLEN
    for ref in (q, gm):
        ref[pl.ds(rows + MAXLEN, beyond), :] = jnp.zeros((beyond, width), ref.dtype)

    def to_prev(i, source, target):
        return pltpu.make_async_remote_copy(
            src_ref=source,
            dst_ref=target,
            send_sem=back_send.at[i],
            recv_sem=back_recv.at[i],
            device_id=device(jnp.where(has_prev, me - 1, me + 1)),
            device_id_type=MESH,
        )

    def gm_part(i, row, height, column, span):
        lanes = pl.ds(column, span)
        return to_prev(
            i, gm.at[pl.ds(row, height), lanes], gm.at[pl.ds(rows + row, height), lanes]
        )

    back_q = to_prev(
        0, proj.at[pl.ds(0, MAXLEN), pl.ds(0, width)], q.at[pl.ds(rows, MAXLEN), :]
    )
    back_second = gm_part(1, BLOCK, MAXLEN - BLOCK, 0, width)
    back_first = [
        gm_part(2 + i, 0, BLOCK, i * piece_width, piece_width) for i in range(PIECES)
    ]
    backs = [back_q, back_second] + back_first

    loads[4].wait()

    base = (me * rows).astype(jnp.float32)
    lane = (lax.broadcasted_iota(jnp.int32, (1, quad), 1) % BLOCK).astype(jnp.float32)
    positions = [base + float(b * BLOCK) + lane for b in range(every)]
    starts = [jnp.zeros((1, quad), jnp.float32) for _ in range(every)]
    carry = jnp.zeros((1, 1), jnp.float32)
    count = lengths.shape[1]
    for first in range(0, count, 128):
        span = min(128, count - first)
        part = lengths[:, first : first + span].astype(jnp.float32)
        upto = lax.broadcasted_iota(jnp.int32, (span, span), 1) <= lax.broadcasted_iota(
            jnp.int32, (span, span), 0
        )
        ends = carry + jnp.sum(jnp.where(upto, part, 0.0), axis=1, keepdims=True)
        carry = carry + jnp.sum(part, axis=1, keepdims=True)
        for b in range(every):
            reached = jnp.max(jnp.where(ends <= positions[b], ends, 0.0), axis=0, keepdims=True)
            starts[b] = jnp.maximum(starts[b], reached)
    offset = lax.broadcasted_iota(jnp.int32, (KEYS, quad), 0).astype(jnp.float32)
    for b in range(every):
        key = offset + (base + float(b * BLOCK - MAXLEN))
        keep = (starts[b] <= key) & (key <= positions[b])
        masks[b] = jnp.where(keep, 1.0, 0.0)

    own_head = (
        lax.broadcasted_iota(jnp.int32, (quad, quad), 0) // BLOCK
        == lax.broadcasted_iota(jnp.int32, (quad, quad), 1) // (quad // QUAD)
    )
    ones[...] = jnp.where(own_head, 1.0, 0.0).astype(ones.dtype)
    sixteenths[...] = jnp.where(own_head, 0.0625, 0.0).astype(ones.dtype)
    head = quad // QUAD
    left_head = lax.broadcasted_iota(jnp.int32, (BLOCK, 2 * head), 1) < head

    def stacked(value, head_mask):
        return jnp.concatenate([value] * QUAD, 0) * head_mask[...]

    def block_rows(b):
        return pl.ds(b * BLOCK, BLOCK)

    def per_head(transposed, values):
        pairs = []
        for p in range(QUAD // 2):
            stack = slice(p * 2 * BLOCK, (p + 1) * 2 * BLOCK)
            lanes = slice(p * 2 * head, (p + 1) * 2 * head)
            both = dot(transposed[:, stack], values[:, lanes], 0, 0)
            pairs.append(jnp.where(left_head, both[:BLOCK], both[BLOCK:]))
        return jnp.concatenate(pairs, 1)

    def reach(b):
        return min(KEYS, MAXLEN + rows - b * BLOCK)

    def forward(b, c):
        span = reach(b)
        keys = kv[pl.ds(b * BLOCK, span), columns(c)]
        queries = stacked(q[block_rows(b), columns(c)], sixteenths)
        h = dot(keys, queries, 1, 1)
        t = jnp.tanh(h)
        kept = (1.0 + t) * masks[b, pl.ds(0, span), :]
        w = (h * kept).astype(weights.dtype)
        weights[b, c, pl.ds(0, span), :] = w
        slopes[b, c, pl.ds(0, span), :] = kept * (1.0 + h * (1.0 - t))
        if b < blocks:
            values = kv[pl.ds(b * BLOCK, span), columns(c, 1)]
            mixed[block_rows(b), columns(c)] = per_head(w, values)

    def normalise(b):
        at = block_rows(b)
        m = mixed[at, :]
        centered = m - jnp.mean(m, axis=1, keepdims=True)
        rstd = lax.rsqrt(jnp.mean(centered * centered, axis=1, keepdims=True) + 1e-05)
        normed = centered * rstd
        d = dy[at, :].astype(jnp.float32)
        result[at, pl.ds(3 * width, width)] = (d * normed).astype(result.dtype)
        dn = d * u[at, :].astype(jnp.float32)
        mean_dn = jnp.mean(dn, axis=1, keepdims=True)
        mean_dnn = jnp.mean(dn * normed, axis=1, keepdims=True)
        gm[at, :] = (rstd * (dn - mean_dn - normed * mean_dnn)).astype(gm.dtype)

    written = set()
    left = {}
    for e in range(MAXLEN // CHUNK, (MAXLEN + rows) // CHUNK):
        users = [b for b in range(every) if b * BLOCK <= e * CHUNK < b * BLOCK + KEYS]
        for c in range(quads):
            for part in range(2):
                left[e, c, part] = len(users)

    def add(b, c, part, row, value):
        for i in range(value.shape[0] // CHUNK):
            key = (row // CHUNK + i, c, part)
            piece = value[i * CHUNK : (i + 1) * CHUNK]
            at = pl.ds(row + i * CHUNK, CHUNK)
            if key in written:
                piece = piece + acc[at, columns(c, part)]
            written.add(key)
            left[key] -= 1
            if left[key]:
                acc[at, columns(c, part)] = piece
            else:
                own = pl.ds(row + i * CHUNK - MAXLEN, CHUNK)
                result[own, columns(c, 1 + part)] = piece.astype(result.dtype)

    def backward(b, c):
        span = reach(b)
        skip = max(0, MAXLEN - b * BLOCK)
        keys = kv[pl.ds(b * BLOCK, span), columns(c)]
        values = kv[pl.ds(b * BLOCK, span), columns(c, 1)]
        queries = stacked(q[block_rows(b), columns(c)], sixteenths)
        grads = stacked(gm[block_rows(b), columns(c)], ones)
        grad_weights = dot(values, grads, 1, 1)
        grad_scores = (grad_weights * slopes[b, c, pl.ds(0, span), :]).astype(jnp.bfloat16)
        add(b, c, 0, b * BLOCK + skip, dot(grad_scores[skip:], queries, 1, 0))
        w = weights[b, c, pl.ds(skip, span - skip), :]
        add(b, c, 1, b * BLOCK + skip, dot(w, grads, 1, 0))
        if b < blocks:
            grad_q = per_head(grad_scores, keys) * 0.0625
            result[block_rows(b), columns(c)] = grad_q.astype(result.dtype)

    def piece(i):
        return range(i * quads // PIECES, (i + 1) * quads // PIECES)

    upper, after = range(2, blocks), range(blocks, every)

    for copy in loads[:2]:
        copy.wait()
    for c in range(quads):
        for b in upper:
            forward(b, c)
    for copy in loads[2:4]:
        copy.wait()
    for b in upper:
        normalise(b)
    for c in range(quads):
        for b in upper:
            backward(b, c)

    @pl.when(has_prev)
    def _():
        back_q.start()
        near.wait_recv()

    for c in range(quads):
        forward(1, c)
    normalise(1)

    @pl.when(has_prev)
    def _():
        back_second.start()

    for i in range(PIECES):

        @pl.when(has_prev)
        def _():
            for copy in far[i]:
                copy.wait_recv()

        for c in piece(i):
            forward(0, c)
    normalise(0)

    @pl.when(has_prev)
    def _():
        for copy in back_first:
            copy.start()

    for b in (1, 0):
        for c in range(quads):
            backward(b, c)

    @pl.when(has_next)
    def _():
        back_q.wait_recv()

    for c in range(quads):
        for b in after:
            forward(b, c)

    @pl.when(has_next)
    def _():
        back_second.wait_recv()

    for c in range(quads):
        backward(blocks + 1, c)

    for i in range(PIECES):

        @pl.when(has_next)
        def _():
            back_first[i].wait_recv()

        for c in piece(i):
            backward(blocks, c)

    @pl.when(has_next)
    def _():
        for copy in halos:
            copy.wait_send()

    @pl.when(has_prev)
    def _():
        for copy in backs:
            copy.wait_send()


def on_device(mesh, projected, grad_gated, lengths):
    rows, width = grad_gated.shape
    quad = QUAD * (width // HEADS)
    quads = width // quad
    blocks = rows // BLOCK + 2
    bf16, f32 = jnp.bfloat16, jnp.float32
    window = rows + MAXLEN
    hbm = pl.BlockSpec(memory_space=pltpu.HBM)
    counts = lengths.reshape(1, -1)
    return pl.pallas_call(
        functools.partial(kernel, mesh.shape["dp"], mesh.shape["shard"]),
        out_shape=jax.ShapeDtypeStruct((rows, 4 * width), bf16),
        in_specs=[hbm, hbm, hbm],
        out_specs=pl.BlockSpec(memory_space=pltpu.VMEM),
        scratch_shapes=[
            pltpu.VMEM(counts.shape, jnp.int32),
            pltpu.VMEM((window, 2 * width), bf16),
            pltpu.VMEM((blocks * BLOCK, width), bf16),
            pltpu.VMEM((rows, width), bf16),
            pltpu.VMEM((rows, width), bf16),
            pltpu.VMEM((rows, width), f32),
            pltpu.VMEM((blocks * BLOCK, width), bf16),
            pltpu.VMEM((blocks, quads, KEYS, quad), bf16),
            pltpu.VMEM((blocks, quads, KEYS, quad), f32),
            pltpu.VMEM((window, 2 * width), f32),
            pltpu.VMEM((quad, quad), bf16),
            pltpu.VMEM((quad, quad), bf16),
            pltpu.VMEM((blocks, KEYS, quad), f32),
            pltpu.SemaphoreType.DMA((5,)),
            pltpu.SemaphoreType.DMA((1 + 2 * PIECES,)),
            pltpu.SemaphoreType.DMA((1 + 2 * PIECES,)),
            pltpu.SemaphoreType.DMA((2 + PIECES,)),
            pltpu.SemaphoreType.DMA((2 + PIECES,)),
        ],
        compiler_params=pltpu.CompilerParams(
            collective_id=0, has_side_effects=True, vmem_limit_bytes=40 * 1024 * 1024
        ),
        cost_estimate=pl.CostEstimate(
            flops=6 * 2 * rows * KEYS * width * QUAD,
            bytes_accessed=rows * width * 2 * 9,
            transcendentals=rows * KEYS * HEADS,
        ),
    )(*(pltpu.with_memory_space_constraint(a, pltpu.HBM) for a in (projected, grad_gated, counts)))


def solution(mesh):
    in_specs = (P(("groups", "dp", "shard"), None), P(("groups", "dp", "shard"), None), P("groups"))
    out_specs = P(("groups", "dp", "shard"), None)
    return jax.shard_map(
        functools.partial(on_device, mesh),
        mesh=mesh, in_specs=in_specs, out_specs=out_specs, check_vma=False,
    )
```
